128 devices in a mesh: db: 16 (over x, y), seq: 8 (over z, core).
Axes of the slice: x: 4, y: 4, z: 4, core: 2. Of those that a mesh axis runs over, the one named last changes fastest.
Arguments:
- hidden: bfloat16 [16384, 4096], P(('db', 'seq')), may hold values from -6 to 6
- grad_out: bfloat16 [16384, 4096], P(('db', 'seq')), may hold values from -24 to 24
- w_query: bfloat16 [4096, 2048], P(None, 'seq'), may hold values from -0.09375 to 0.09375
- w_key: bfloat16 [896, 2048], P(None, 'seq'), may hold values from -0.1875 to 0.1875
- w_value: bfloat16 [896, 2048], P(None, 'seq'), may hold values from -0.1875 to 0.1875
- w_out: bfloat16 [2048, 4096], P('seq'), may hold values from -0.125 to 0.125
- database: bfloat16 [4096, 128, 896], P('db', 'seq'), may hold values from -6 to 6
- nbr_shard: int32 [256, 2], P('db'), may hold values from 0 to 15, all different within a row; in each aligned block of 16 rows (0 to 15, 16 to 31, ...) at most 3 rows name the same one
- nbr_row: int32 [256, 2], P('db'), may hold values from 0 to 255
Outputs:
- grad_hidden: bfloat16 [16384, 4096], P(('db', 'seq'))
- grad_w_query: float32 [4096, 2048], P('db', 'seq')
- grad_w_key: float32 [896, 2048], P('db', 'seq')
- grad_w_value: float32 [896, 2048], P('db', 'seq')
- grad_w_out: float32 [2048, 4096], P('seq', 'db')
The draws below stay inside these ranges and needn't reach their ends.
Inputs may be any that keep to these rules, and one draw needn't show every extreme that they name: `nbr_shard`: the 2 shards of one span differ. Among the spans of one sequence (aligned blocks of 16 rows) no shard is named more than 3 times, a bound that some block reaches.
All inputs are finite; a program needn't handle non-finite values.
Results may differ from the reference program's by a relative error of at most 0.022.
Values may be sent and summed in bfloat16 or wider, within the bound.
No kernel may reach another device: no remote copies, remote signals or barrier semaphores. Data moves between devices by JAX's collectives and lax.ppermute only.
A program may use at most 128 MiB of HBM per device.

```python
import math
import jax
import jax.numpy as jnp
import numpy as np
from jax import lax

D = 4096
HEADS = 16
HEAD_SIZE = 128
ENC_WIDTH = 896
SPAN_LEN = 64
NEIGHBOURS = 2
NEIGHBOUR_LEN = 128
CAPACITY = 3
SHARD_ROWS = 256
HEAD_WIDTH = 2048
GROUP_TOKENS = 1024
GROUP_SPANS = 16
TOKENS = 16384
SPANS = 256
DB_ROWS = 4096
N_DB = 16
N_SEQ = 8


def with_ends(result, own_key, low, largest):
    extent = result.shape
    spot = [jax.random.randint(jax.random.fold_in(own_key, axis), (), 0, extent[axis]) for axis in range(len(extent))]
    result = result.at[tuple(spot)].set(low)
    longest = extent.index(max(extent))
    spot[longest] = (spot[longest] + 1) % extent[longest]
    return result.at[tuple(spot)].set(largest)


def block_scale(key, extent, cuts, smallest, top_value):
    def one(dim, blocks):
        draws = jax.random.uniform(jax.random.fold_in(jax.random.fold_in(key, 6), dim), (blocks,), jnp.float32, smallest / len(cuts), top_value / len(cuts))
        return jnp.repeat(jnp.exp(draws), extent[dim] // blocks).reshape((-1,) + (1,) * (len(extent) - dim - 1))

    loudness = one(*cuts[0])
    for cut in cuts[1:]:
        loudness = loudness * one(*cut)
    return loudness


def deal_out(rng, own, number, rows, count, top, limit, lean):
    sequence = jax.random.permutation(rng, count)
    heavy_load, usual = shares(count, rows * top, limit, lean, True), shares(count, rows * top, limit, lean, False)
    places = jnp.arange(count)

    def named(tallies, offset_by):
        used = int((tallies > 0).sum())
        fixed = max(1, used // 4)
        moved = fixed + (places - fixed + offset_by * (used - fixed)) % max(1, count - fixed)
        return jnp.zeros((count,), jnp.int32).at[sequence[jnp.where(places < fixed, places, moved)]].set(jnp.asarray(tallies, jnp.int32))

    tallies = jnp.where(number % 4 == 0, named(heavy_load, number // 4), named(usual, number - number // 4 - 1))
    mixed = jax.random.permutation(jax.random.fold_in(own, 3), count)
    giver, taker = mixed[0:count // 2 * 2:2], mixed[1:count // 2 * 2:2]
    room = jnp.minimum(tallies[giver] - 1, limit - tallies[taker]) // 2
    room = jnp.where((giver == sequence[0]) | (taker == sequence[0]) | (tallies[taker] == 0), 0, jnp.maximum(room, 0))
    moved = jax.random.randint(jax.random.fold_in(own, 4), (count // 2,), 0, 1 << 20) % (room + 1)
    tallies = tallies.at[giver].add(-moved).at[taker].add(moved)
    items = jnp.searchsorted(jnp.cumsum(tallies), jnp.arange(rows * top), side="right").astype(jnp.int32)
    table = items.reshape(top, rows).T
    table = table[jax.random.permutation(jax.random.fold_in(own, 1), rows)]
    offset_by = jax.random.randint(jax.random.fold_in(own, 2), (rows, 1), 0, top)
    return jnp.take_along_axis(table, (jnp.arange(top)[None, :] + offset_by) % top, axis=1)


def shares(number_of, total, limit, lean, full):
    loads = [(1 << 20) // math.isqrt(rank ** lean) + 1 for rank in range(1, number_of + 1)]
    largest = limit if full else min(limit, max(-(-total // number_of), total * loads[0] // sum(loads)))
    least = 1 if total - largest >= number_of - 1 else 0
    given, surplus = [largest] + [least] * (number_of - 1), total - largest - least * (number_of - 1)
    while surplus > 0:
        candidates = [i for i in range(1, number_of) if given[i] < largest] or [i for i in range(1, number_of) if given[i] < limit]
        whole, remaining = sum([loads[i] for i in candidates]), surplus
        for i in candidates:
            more = min(limit - given[i], max(1, remaining * loads[i] // whole), surplus)
            given[i] = given[i] + more
            surplus = surplus - more
    return np.array(given)


def normal_values(stream_key, extent, spread, bound, shards=(), held_as=jnp.bfloat16):
    result = spread * jax.random.normal(stream_key, extent, jnp.float32)
    if shards:
        result = result * block_scale(stream_key, extent, shards, -0.22, 0.18)
    return jnp.clip(result, -bound, bound).astype(held_as)


def setup_inputs(seed: int = 0) -> dict:
    splits = jax.random.split(jax.random.key(seed), 10)
    hidden = normal_values(splits[0], (TOKENS, D), 1.0, 6.0, ((0, 128),))
    grad_out = normal_values(splits[1], (TOKENS, D), 4.0, 24.0, ((0, 128),))
    w_query = normal_values(splits[2], (D, HEAD_WIDTH), D ** -0.5, 0.09375, ((1, 8),))
    w_key = normal_values(splits[3], (ENC_WIDTH, HEAD_WIDTH), ENC_WIDTH ** -0.5, 0.1875, ((1, 8),))
    w_value = normal_values(splits[4], (ENC_WIDTH, HEAD_WIDTH), ENC_WIDTH ** -0.5, 0.1875, ((1, 8),))
    w_out = normal_values(splits[5], (HEAD_WIDTH, D), HEAD_WIDTH ** -0.5, 0.125, ((0, 8),))
    database = normal_values(splits[6], (DB_ROWS, NEIGHBOUR_LEN, ENC_WIDTH), 1.0, 6.0, ((0, 16), (1, 8)))
    nbr_shard_keys = jax.random.split(jax.random.fold_in(splits[7], 1), SPANS // GROUP_SPANS)
    nbr_shard_turns = jax.random.permutation(jax.random.fold_in(splits[7], 3), SPANS // GROUP_SPANS)
    nbr_shard = jax.vmap(lambda own, number: deal_out(jax.random.fold_in(splits[7], 2), own, number, GROUP_SPANS, N_DB, NEIGHBOURS, CAPACITY, 2))(nbr_shard_keys, nbr_shard_turns).reshape((SPANS, NEIGHBOURS))
    nbr_row = with_ends(jax.random.randint(splits[8], (SPANS, NEIGHBOURS), 0, SHARD_ROWS), jax.random.fold_in(splits[8], 1), 0, SHARD_ROWS - 1).astype(jnp.int32)
    return dict(hidden=hidden, grad_out=grad_out, w_query=w_query, w_key=w_key, w_value=w_value, w_out=w_out, database=database, nbr_shard=nbr_shard, nbr_row=nbr_row)


def shifted(rows, heads):
    tail = rows[SPAN_LEN - 1:]
    filler = jnp.zeros((SPAN_LEN - 1, rows.shape[1]), rows.dtype)
    joined = jnp.concatenate([tail, filler], axis=0)
    return joined.reshape(-1, SPAN_LEN, heads, HEAD_SIZE)


def unshifted(blocks):
    width = blocks.shape[2] * blocks.shape[3]
    rows = blocks.reshape(-1, width)
    filler = jnp.zeros((SPAN_LEN - 1, width), rows.dtype)
    return jnp.concatenate([filler, rows[:rows.shape[0] - SPAN_LEN + 1]], axis=0)


def group_pass(hidden_rows, grad_rows, shard_ids, row_ids, w_query, w_key, w_value, w_out, database):
    scale = HEAD_SIZE ** -0.5
    rescale = TOKENS ** -0.5
    index = (shard_ids * SHARD_ROWS + row_ids).reshape(-1).astype(jnp.int32)
    encoded = jnp.take(database, index, axis=0)
    flat = encoded.reshape(-1, ENC_WIDTH)
    keys = jnp.dot(flat, w_key, preferred_element_type=jnp.float32).astype(jnp.bfloat16)
    values = jnp.dot(flat, w_value, preferred_element_type=jnp.float32).astype(jnp.bfloat16)
    query = jnp.dot(hidden_rows, w_query, preferred_element_type=jnp.float32).astype(jnp.bfloat16)
    query_blocks = shifted(query, HEADS).astype(jnp.float32)
    key_blocks = keys.reshape(-1, NEIGHBOURS * NEIGHBOUR_LEN, HEADS, HEAD_SIZE).astype(jnp.float32)
    value_blocks = values.reshape(-1, NEIGHBOURS * NEIGHBOUR_LEN, HEADS, HEAD_SIZE).astype(jnp.float32)
    scores = jnp.einsum('cqhe,ckhe->chqk', query_blocks, key_blocks) * scale
    expo = jnp.exp(scores)
    probs = expo / jnp.sum(expo, axis=-1, keepdims=True)
    probs_low = probs.astype(jnp.bfloat16).astype(jnp.float32)
    context_blocks = jnp.einsum('chqk,ckhe->cqhe', probs_low, value_blocks).astype(jnp.bfloat16)
    context = unshifted(context_blocks)
    grad_context = jnp.dot(grad_rows, w_out.T, preferred_element_type=jnp.float32).astype(jnp.bfloat16)
    out_term = jnp.dot(context.T, grad_rows, preferred_element_type=jnp.float32)
    gctx_blocks = shifted(grad_context, HEADS).astype(jnp.float32)
    grad_probs = jnp.einsum('cqhe,ckhe->chqk', gctx_blocks, value_blocks)
    inner = jnp.sum(probs * grad_probs, axis=-1, keepdims=True)
    grad_scores = (probs * (grad_probs - inner) * scale).astype(jnp.bfloat16).astype(jnp.float32)
    gq_blocks = jnp.einsum('chqk,ckhe->cqhe', grad_scores, key_blocks).astype(jnp.bfloat16)
    grad_keys = jnp.einsum('chqk,cqhe->ckhe', grad_scores, query_blocks).astype(jnp.bfloat16)
    grad_values = jnp.einsum('chqk,cqhe->ckhe', probs_low, gctx_blocks).astype(jnp.bfloat16)
    grad_query = unshifted(gq_blocks)
    block_width = HEAD_WIDTH // N_SEQ
    query_parts = grad_query.reshape(GROUP_TOKENS, N_SEQ, block_width).astype(jnp.float32)
    weight_parts = w_query.reshape(D, N_SEQ, block_width).astype(jnp.float32)
    pieces = jnp.einsum('tsw,dsw->std', query_parts, weight_parts).astype(jnp.bfloat16)
    grad_in = jnp.sum(pieces.astype(jnp.float32), axis=0).astype(jnp.bfloat16)
    part_query = (jnp.dot(hidden_rows.T, grad_query, preferred_element_type=jnp.float32) * rescale).astype(jnp.bfloat16)
    part_key = (jnp.dot(flat.T, grad_keys.reshape(-1, HEAD_WIDTH), preferred_element_type=jnp.float32) * rescale).astype(jnp.bfloat16)
    part_value = (jnp.dot(flat.T, grad_values.reshape(-1, HEAD_WIDTH), preferred_element_type=jnp.float32) * rescale).astype(jnp.bfloat16)
    part_out = (out_term * rescale).astype(jnp.bfloat16)
    return grad_in, (part_query, part_key, part_value, part_out)


def reference(hidden, grad_out, w_query, w_key, w_value, w_out, database, nbr_shard, nbr_row):
    groups = (hidden.reshape(N_DB, GROUP_TOKENS, D),
              grad_out.reshape(N_DB, GROUP_TOKENS, D),
              nbr_shard.reshape(N_DB, GROUP_SPANS, NEIGHBOURS),
              nbr_row.reshape(N_DB, GROUP_SPANS, NEIGHBOURS))
    start = (jnp.zeros((D, HEAD_WIDTH), jnp.float32),
             jnp.zeros((ENC_WIDTH, HEAD_WIDTH), jnp.float32),
             jnp.zeros((ENC_WIDTH, HEAD_WIDTH), jnp.float32),
             jnp.zeros((HEAD_WIDTH, D), jnp.float32))

    def advance(totals, items):
        grad_in, parts = group_pass(items[0], items[1], items[2], items[3], w_query, w_key, w_value, w_out, database)
        updated = tuple(total + part.astype(jnp.float32) for total, part in zip(totals, parts))
        return updated, grad_in

    totals, grad_rows = lax.scan(advance, start, groups)
    return grad_rows.reshape(TOKENS, D), totals[0], totals[1], totals[2], totals[3]
```

```python
import functools

import jax
import jax.numpy as jnp
from jax import lax
from jax.experimental import pallas as pl
from jax.experimental.pallas import tpu as pltpu
from jax.sharding import PartitionSpec as P

HEAD_SIZE = 128
ENC_WIDTH = 896
SPAN_LEN = 64
NEIGHBOURS = 2
CAPACITY = 3
SIDE = 4
CHIPS = 4
CORES = 2
MB = 1 << 20
F32 = jnp.float32
BF16 = jnp.bfloat16


def along_xy(array, dx, dy):
    pairs = [
        (x * SIDE + y, ((x + dx) % SIDE) * SIDE + (y + dy) % SIDE)
        for x in range(SIDE)
        for y in range(SIDE)
    ]
    return lax.ppermute(array, "db", pairs)


def along_z(array, dz):
    pairs = [
        (z * CORES + c, ((z + dz) % CHIPS) * CORES + c) for z in range(CHIPS) for c in range(CORES)
    ]
    return lax.ppermute(array, "seq", pairs)


def other_core(array):
    pairs = [(z * CORES + c, z * CORES + 1 - c) for z in range(CHIPS) for c in range(CORES)]
    return lax.ppermute(array, "seq", pairs)


def gather_seq(block):
    half = block.shape[0] // 2
    before = along_z(block, 1)
    after = along_z(block, -1)
    far_low = along_z(before[:half], 1)
    far_high = along_z(after[half:], -1)
    far = jnp.concatenate([far_low, far_high], axis=0)
    pieces = []
    for piece in (block, after, far, before):
        pieces += [piece, other_core(piece)]
    return pieces


def pick(array, index, axis):
    return lax.dynamic_index_in_dim(array, index, axis, keepdims=False)


def reduce_over_xy(first, second, x, y):
    def step(terms, axis, place, move):
        total = pick(terms, place, axis).astype(F32)
        for i in range(1, SIDE):
            sent = pick(terms, (place + i) % SIDE, axis)
            total = total + move(sent, i).astype(F32)
        return total

    def move_x(array, i):
        return along_xy(array, i, 0)

    def move_y(array, i):
        return along_xy(array, 0, i)

    first = step(first, 0, x, move_x).astype(BF16)
    second = step(second, 1, y, move_y).astype(BF16)
    return step(first, 0, y, move_y), step(second, 0, x, move_x)


def nt(a, b):
    return lax.dot_general(a, b, (((1,), (1,)), ((), ())), preferred_element_type=F32)


def tn(a, b):
    return lax.dot_general(a, b, (((0,), (0,)), ((), ())), preferred_element_type=F32)


def attention_kernel(places, query, gctx, *refs):
    kv = refs[:8]
    ctx_out, gq_out, gkv_out = refs[8:11]
    q_s, g_s, c_s, gq_s = refs[11:]
    scale = HEAD_SIZE ** (-0.5)
    rows = query.shape[1]
    count = query.shape[0]
    width = query.shape[2]
    heads = width // HEAD_SIZE
    spans = kv[0].shape[0]
    part = kv[0].shape[1]
    total = count * rows
    for p in range(count):
        r = places[p]
        q_s[pl.ds(1 + p * rows, rows), :] = query[r].astype(F32)
        g_s[pl.ds(1 + p * rows, rows), :] = gctx[r].astype(F32)
    q_s[pl.ds(total + 1, SPAN_LEN - 1), :] = jnp.zeros((SPAN_LEN - 1, width), F32)
    g_s[pl.ds(total + 1, SPAN_LEN - 1), :] = jnp.zeros((SPAN_LEN - 1, width), F32)
    c_s[pl.ds(0, SPAN_LEN), :] = jnp.zeros((SPAN_LEN, width), F32)
    gq_s[pl.ds(0, SPAN_LEN), :] = jnp.zeros((SPAN_LEN, width), F32)

    def span(c, carry):
        at = pl.ds(pl.multiple_of((c + 1) * SPAN_LEN, SPAN_LEN), SPAN_LEN)
        both = jnp.concatenate([ref[c] for ref in kv], axis=0)
        q = q_s[at, :].astype(BF16)
        g = g_s[at, :].astype(BF16)
        for h in range(heads):
            lanes = slice(h * HEAD_SIZE, (h + 1) * HEAD_SIZE)
            vlanes = slice(width + h * HEAD_SIZE, width + (h + 1) * HEAD_SIZE)
            qh, gh, k, v = q[:, lanes], g[:, lanes], both[:, lanes], both[:, vlanes]
            expo = jnp.exp(nt(qh, k) * scale)
            probs = expo * (1.0 / jnp.sum(expo, axis=-1, keepdims=True))
            low = probs.astype(BF16)
            c_s[at, lanes] = jnp.dot(low, v, preferred_element_type=F32)
            gp = nt(gh, v)
            inner = jnp.sum(probs * gp, axis=-1, keepdims=True)
            gs = (probs * (gp - inner) * scale).astype(BF16)
            gq_s[at, lanes] = jnp.dot(gs, k, preferred_element_type=F32)
            gk = tn(gs, qh).astype(BF16)
            gv = tn(low, gh).astype(BF16)
            for p in range(8):
                gkv_out[p, c, :, lanes] = gk[p * part : (p + 1) * part]
                gkv_out[p, c, :, vlanes] = gv[p * part : (p + 1) * part]
        return carry

    lax.fori_loop(0, spans, span, 0, unroll=2)
    for p in range(count):
        r = places[p]
        ctx_out[r] = c_s[pl.ds(1 + p * rows, rows), :].astype(BF16)
        gq_out[r] = gq_s[pl.ds(1 + p * rows, rows), :].astype(BF16)


def attention(places, query, gctx, kv):
    count, rows, width = query.shape
    total = count * rows
    spans, part, both = kv[0].shape
    vmem = pl.BlockSpec(memory_space=pltpu.VMEM)
    scratch = pltpu.VMEM((total + SPAN_LEN, width), F32)
    flops = 14 * total * both // 2 * 256
    return pl.pallas_call(
        attention_kernel,
        out_shape=(
            jax.ShapeDtypeStruct((count, rows, width), BF16),
            jax.ShapeDtypeStruct((count, rows, width), BF16),
            jax.ShapeDtypeStruct((8, spans, part, both), BF16),
        ),
        in_specs=[pl.BlockSpec(memory_space=pltpu.SMEM)] + [vmem] * 10,
        out_specs=(vmem, vmem, vmem),
        scratch_shapes=[scratch] * 4,
        compiler_params=pltpu.CompilerParams(vmem_limit_bytes=40 * MB),
        cost_estimate=pl.CostEstimate(
            flops=flops, bytes_accessed=10 * MB, transcendentals=spans * 64 * 512
        ),
        name="attention",
    )(places, query, gctx, *kv)


def weight_kernel(rescale, *refs):
    rows, others = refs[0], refs[1:9]
    out, turned = refs[9:]

    @pl.when(pl.program_id(0) == 0)
    def _():
        for r in range(8):
            turned[:, pl.ds(r * rows.shape[1], rows.shape[1])] = rows[r].T

    other = jnp.concatenate([ref[...] for ref in others], axis=0)
    term = jnp.dot(turned[...], other, preferred_element_type=F32) * rescale
    term = term.astype(BF16)
    for b in range(out.shape[0]):
        out[b] = term[:, b * out.shape[2] : (b + 1) * out.shape[2]]


def weight_term(rows, others, rescale, name):
    count, tokens, width = rows.shape
    d = others[0].shape[1]
    blocks = SIDE * SIDE
    per = d // blocks
    step = 2
    return pl.pallas_call(
        functools.partial(weight_kernel, rescale),
        grid=(blocks // step,),
        in_specs=[pl.BlockSpec((count, tokens, width), lambda i: (0, 0, 0))]
        + [pl.BlockSpec((tokens, step * per), lambda i: (0, i))] * 8,
        out_specs=pl.BlockSpec((step, width, per), lambda i: (i, 0, 0)),
        out_shape=jax.ShapeDtypeStruct((blocks, width, per), BF16),
        scratch_shapes=[pltpu.VMEM((width, count * tokens), BF16)],
        compiler_params=pltpu.CompilerParams(vmem_limit_bytes=32 * MB),
        cost_estimate=pl.CostEstimate(
            flops=2 * count * tokens * width * d,
            bytes_accessed=2 * d * (count * tokens + width),
            transcendentals=0,
        ),
        name=name,
    )(rows, *others)


def encoding_kernel(rescale, *refs):
    encs, grads = refs[:8], refs[8]
    out = refs[9]
    held, sems, total = refs[10:]
    copies = [pltpu.make_async_copy(encs[p], held.at[p], sems.at[p]) for p in range(8)]
    for copy in copies:
        copy.start()
    for p in range(8):
        copies[p].wait()
        term = tn(grads[p], held[p])
        if p == 0:
            total[...] = term
        else:
            total[...] += term
    out[...] = (total[...] * rescale).T.astype(BF16)


def encoding_term(encs, grads, rescale):
    rows, width = encs[0].shape
    both = grads.shape[2]
    return pl.pallas_call(
        functools.partial(encoding_kernel, rescale),
        in_specs=[pl.BlockSpec(memory_space=pl.ANY)] * 8 + [pl.BlockSpec(memory_space=pltpu.VMEM)],
        out_specs=pl.BlockSpec(memory_space=pltpu.VMEM),
        out_shape=jax.ShapeDtypeStruct((width, both), BF16),
        scratch_shapes=[
            pltpu.VMEM((8, rows, width), BF16),
            pltpu.SemaphoreType.DMA((8,)),
            pltpu.VMEM((both, width), F32),
        ],
        compiler_params=pltpu.CompilerParams(vmem_limit_bytes=32 * MB),
        cost_estimate=pl.CostEstimate(
            flops=2 * 8 * rows * width * both, bytes_accessed=12 * MB, transcendentals=0
        ),
        name="encoding_term",
    )(*encs, grads)


def fetch_encodings(database, nbr_shard, nbr_row, x, y):
    requests = nbr_shard.shape[0] * NEIGHBOURS
    slice_len = database.shape[1]
    half = slice_len // 2
    shard_flat = nbr_shard.reshape(requests)
    row_flat = nbr_row.reshape(requests)
    mine = jnp.stack([shard_flat, row_flat]).astype(jnp.int32)
    line = jnp.stack([mine] + [along_xy(mine, SIDE - i, 0) for i in range(1, SIDE)])
    tables = jnp.stack([line] + [along_xy(line, 0, SIDE - j) for j in range(1, SIDE)], axis=1)
    me = x * SIDE + y
    wanted = tables[:, :, 0] == me
    order = jnp.arange(requests, dtype=jnp.int32)
    before = (order[None, :] < order[:, None]).astype(F32)
    slot = jnp.einsum("ijs,rs->ijr", wanted.astype(F32), before)
    slots = jnp.arange(CAPACITY, dtype=jnp.int32)
    chosen = wanted[:, :, None, :] & (
        slot[:, :, None, :].astype(jnp.int32) == slots[None, None, :, None]
    )
    rows = jnp.sum(jnp.where(chosen, tables[:, :, 1][:, :, None, :], 0), axis=3)
    served = jnp.take(database, rows.reshape(-1), axis=0)
    served = served.reshape(SIDE, SIDE, CAPACITY, slice_len, ENC_WIDTH)
    low, high = served[:, :, :, :half], served[:, :, :, half:]
    low = jnp.stack([low[0]] + [along_xy(low[i], i, 0) for i in range(1, SIDE)])
    low = jnp.stack([low[:, 0]] + [along_xy(low[:, j], 0, j) for j in range(1, SIDE)], axis=1)
    high = jnp.stack([high[:, 0]] + [along_xy(high[:, j], 0, j) for j in range(1, SIDE)], axis=1)
    high = jnp.stack([high[0]] + [along_xy(high[i], i, 0) for i in range(1, SIDE)])
    same = (shard_flat[:, None] == shard_flat[None, :]) & (order[None, :] < order[:, None])
    slot_index = jnp.sum(same.astype(jnp.int32), axis=1)
    away = ((x - shard_flat // SIDE) % SIDE) * SIDE + (y - shard_flat % SIDE) % SIDE
    places = away * CAPACITY + slot_index
    low = jnp.take(low.reshape(-1, half, ENC_WIDTH), places, axis=0)
    high = jnp.take(high.reshape(-1, half, ENC_WIDTH), places, axis=0)
    return jnp.concatenate([low, high], axis=1).reshape(requests * slice_len, ENC_WIDTH)


def per_device(hidden, grad_out, w_query, w_key, w_value, w_out, database, nbr_shard, nbr_row):
    db = lax.axis_index("db")
    seq = lax.axis_index("seq")
    x, y = db // SIDE, db % SIDE
    z, core = seq // CORES, seq % CORES
    spans = nbr_shard.shape[0]
    width = w_query.shape[1]
    token_rows = hidden.shape[0]
    total_tokens = token_rows * lax.axis_size("db") * lax.axis_size("seq")
    rescale = float(total_tokens) ** (-0.5)
    block = jnp.arange(CHIPS * CORES, dtype=jnp.int32)
    places = ((block // CORES - z) % CHIPS) * CORES + (block % CORES + core) % CORES

    hidden_all = gather_seq(hidden)
    w_both = jnp.concatenate([w_query, other_core(w_query)], axis=1)
    query = jnp.stack(
        [jnp.dot(piece, w_query, preferred_element_type=F32).astype(BF16) for piece in hidden_all]
    )
    grad_all = gather_seq(grad_out)
    gctx = jnp.stack([nt(piece, w_out).astype(BF16) for piece in grad_all])
    encoded = fetch_encodings(database, nbr_shard, nbr_row, x, y)
    enc_all = gather_seq(encoded)
    w_kv = jnp.concatenate([w_key, w_value], axis=1)
    kv = [
        jnp.dot(piece, w_kv, preferred_element_type=F32).astype(BF16).reshape(spans, -1, 2 * width)
        for piece in enc_all
    ]
    context, grad_query, grad_kv = attention(places, query, gctx, kv)

    paired = grad_query.reshape(CHIPS, CORES, token_rows, width)
    joined = jnp.concatenate([paired[:, 0], other_core(paired[:, 1])], axis=2)
    half = token_rows // 2

    def share(k):
        return nt(joined[k], w_both)

    far = share(2).astype(BF16)
    from_before = along_z(far[:half], 1).astype(F32)
    from_after = along_z(far[half:], -1).astype(F32)
    up = share(1)
    up = jnp.concatenate([up[:half] + from_before, up[half:]], axis=0).astype(BF16)
    down = share(3)
    down = jnp.concatenate([down[:half], down[half:] + from_after], axis=0).astype(BF16)
    grad_hidden = (
        share(0) + along_z(up, 1).astype(F32) + along_z(down, -1).astype(F32)
    ).astype(BF16)

    out_term = weight_term(context, grad_all, rescale, "out_term")
    out_term = out_term.reshape(SIDE, SIDE, width, -1)
    kv_term = encoding_term(enc_all, grad_kv.reshape(8, -1, 2 * width), rescale)
    kv_term = kv_term.reshape(SIDE, SIDE, -1, 2 * width)
    cut = width // 2
    first, second = reduce_over_xy(
        jnp.concatenate([out_term[:, :, :cut], kv_term[..., :width]], axis=2),
        jnp.concatenate([out_term[:, :, cut:], kv_term[..., width:]], axis=2),
        x,
        y,
    )
    grad_w_out = jnp.concatenate([first[:cut], second[:cut]], axis=0)
    grad_w_key, grad_w_value = first[cut:], second[cut:]
    query_term = weight_term(grad_query, hidden_all, rescale, "query_term")
    query_term = query_term.reshape(SIDE, SIDE, width, -1)
    first, second = reduce_over_xy(query_term[:, :, :cut], query_term[:, :, cut:], x, y)
    grad_w_query = jnp.concatenate([first, second], axis=0).T
    return grad_hidden, grad_w_query, grad_w_key, grad_w_value, grad_w_out


def solution(mesh):
    return jax.shard_map(
        per_device,
        mesh=mesh,
        in_specs=(
            P(("db", "seq"), None),
            P(("db", "seq"), None),
            P(None, "seq"),
            P(None, "seq"),
            P(None, "seq"),
            P("seq", None),
            P("db", "seq", None),
            P("db", None),
            P("db", None),
        ),
        out_specs=(
            P(("db", "seq"), None),
            P("db", "seq"),
            P("db", "seq"),
            P("db", "seq"),
            P("seq", "db"),
        ),
        check_vma=False,
    )
```

```python
import functools

import jax
import jax.numpy as jnp
from jax import lax
from jax.experimental import pallas as pl
from jax.experimental.pallas import tpu as pltpu
from jax.sharding import PartitionSpec as P

HEAD_SIZE = 128
ENC_WIDTH = 896
SPAN_LEN = 64
NEIGHBOURS = 2
CAPACITY = 3
SIDE = 4
CHIPS = 4
CORES = 2
MB = 1 << 20
F32 = jnp.float32
BF16 = jnp.bfloat16


def line_pairs(step):
    def pairs(phase):
        out = []
        for x in range(SIDE):
            for y in range(SIDE):
                for z in range(CHIPS):
                    for c in range(CORES):
                        dx, dy = (step, 0) if c == phase else (0, step)
                        there = ((x + dx) % SIDE) * SIDE + (y + dy) % SIDE
                        seq = z * CORES + c
                        out.append(((x * SIDE + y) * CHIPS * CORES + seq, there * CHIPS * CORES + seq))
        return out

    return pairs


def spread(array, step, phase):
    return lax.ppermute(array, ("db", "seq"), line_pairs(step)(phase))


def along_x(array, step):
    pairs = [
        (x * SIDE + y, ((x + step) % SIDE) * SIDE + y) for x in range(SIDE) for y in range(SIDE)
    ]
    return lax.ppermute(array, "db", pairs)


def along_y(array, step):
    pairs = [
        (x * SIDE + y, x * SIDE + (y + step) % SIDE) for x in range(SIDE) for y in range(SIDE)
    ]
    return lax.ppermute(array, "db", pairs)


def along_z(array, way=1, flip=0):
    pairs = [
        (z * CORES + c, ((z + way * (1 - 2 * c)) % CHIPS) * CORES + (c ^ flip))
        for z in range(CHIPS)
        for c in range(CORES)
    ]
    return lax.ppermute(array, "seq", pairs)


def other_core(array):
    pairs = [(z * CORES + c, z * CORES + 1 - c) for z in range(CHIPS) for c in range(CORES)]
    return lax.ppermute(array, "seq", pairs)


def after(array, *others):
    return lax.optimization_barrier((array,) + others)[0]


def arrange(block, low, high, far):
    return [
        block,
        far,
        high,
        other_core(low),
        other_core(block),
        other_core(far),
        other_core(high),
        low,
    ]


def piece_blocks(z, core):
    s = 1 - 2 * core
    chips = jnp.stack([0 * s, 0 * s + 2, s, s, 0 * s, 0 * s + 2, -s, -s])
    cores = jnp.stack([core, core, core, 1 - core, 1 - core, 1 - core, 1 - core, core])
    return ((z + chips) % CHIPS) * CORES + cores


def reduce_lines(terms, phase):
    total = terms[0].astype(F32)
    for i in range(1, SIDE):
        total = total + spread(terms[i], i, phase).astype(F32)
    return total


def reduce_over_db(terms):
    total = reduce_lines(terms, 0).astype(BF16)
    return reduce_lines([total[j] for j in range(SIDE)], 1)


def nt(a, b):
    return lax.dot_general(a, b, (((1,), (1,)), ((), ())), preferred_element_type=F32)


def tn(a, b):
    return lax.dot_general(a, b, (((0,), (0,)), ((), ())), preferred_element_type=F32)


def attention_kernel(places, query, gctx, *refs):
    kv = refs[:8]
    ctx_out, gq_out, gkv_out = refs[8:11]
    q_s, g_s, c_s, gq_s = refs[11:]
    scale = HEAD_SIZE ** (-0.5)
    rows = query.shape[1]
    count = query.shape[0]
    width = query.shape[2]
    heads = width // HEAD_SIZE
    spans = kv[0].shape[0]
    part = kv[0].shape[1]
    total = count * rows
    for p in range(count):
        r = places[p]
        q_s[pl.ds(1 + p * rows, rows), :] = query[r].astype(F32)
        g_s[pl.ds(1 + p * rows, rows), :] = gctx[r].astype(F32)
    q_s[pl.ds(total + 1, SPAN_LEN - 1), :] = jnp.zeros((SPAN_LEN - 1, width), F32)
    g_s[pl.ds(total + 1, SPAN_LEN - 1), :] = jnp.zeros((SPAN_LEN - 1, width), F32)
    c_s[pl.ds(0, SPAN_LEN), :] = jnp.zeros((SPAN_LEN, width), F32)
    gq_s[pl.ds(0, SPAN_LEN), :] = jnp.zeros((SPAN_LEN, width), F32)

    def span(c, carry):
        at = pl.ds(pl.multiple_of((c + 1) * SPAN_LEN, SPAN_LEN), SPAN_LEN)
        both = jnp.concatenate([ref[c] for ref in kv], axis=0)
        q = q_s[at, :].astype(BF16)
        g = g_s[at, :].astype(BF16)
        for h in range(heads):
            lanes = slice(h * HEAD_SIZE, (h + 1) * HEAD_SIZE)
            vlanes = slice(width + h * HEAD_SIZE, width + (h + 1) * HEAD_SIZE)
            qh, gh, k, v = q[:, lanes], g[:, lanes], both[:, lanes], both[:, vlanes]
            expo = jnp.exp(nt(qh, k) * scale)
            probs = expo * (1.0 / jnp.sum(expo, axis=-1, keepdims=True))
            low = probs.astype(BF16)
            c_s[at, lanes] = jnp.dot(low, v, preferred_element_type=F32)
            gp = nt(gh, v)
            inner = jnp.sum(probs * gp, axis=-1, keepdims=True)
            gs = (probs * (gp - inner) * scale).astype(BF16)
            gq_s[at, lanes] = jnp.dot(gs, k, preferred_element_type=F32)
            gk = tn(gs, qh).astype(BF16)
            gv = tn(low, gh).astype(BF16)
            for p in range(8):
                gkv_out[p, c, :, lanes] = gk[p * part : (p + 1) * part]
                gkv_out[p, c, :, vlanes] = gv[p * part : (p + 1) * part]
        return carry

    lax.fori_loop(0, spans, span, 0, unroll=2)
    for p in range(count):
        r = places[p]
        ctx_out[r] = c_s[pl.ds(1 + p * rows, rows), :].astype(BF16)
        gq_out[r] = gq_s[pl.ds(1 + p * rows, rows), :].astype(BF16)


def attention(places, query, gctx, kv):
    count, rows, width = query.shape
    total = count * rows
    spans, part, both = kv[0].shape
    vmem = pl.BlockSpec(memory_space=pltpu.VMEM)
    scratch = pltpu.VMEM((total + SPAN_LEN, width), F32)
    flops = 14 * total * both // 2 * 256
    return pl.pallas_call(
        attention_kernel,
        out_shape=(
            jax.ShapeDtypeStruct((count, rows, width), BF16),
            jax.ShapeDtypeStruct((count, rows, width), BF16),
            jax.ShapeDtypeStruct((8, spans, part, both), BF16),
        ),
        in_specs=[pl.BlockSpec(memory_space=pltpu.SMEM)] + [vmem] * 10,
        out_specs=(vmem, vmem, vmem),
        scratch_shapes=[scratch] * 4,
        compiler_params=pltpu.CompilerParams(vmem_limit_bytes=16 * MB),
        cost_estimate=pl.CostEstimate(
            flops=flops, bytes_accessed=10 * MB, transcendentals=spans * 64 * 512
        ),
        name="attention",
    )(places, query, gctx, *kv)


def weight_kernel(rescale, with_encodings, blocks, rows, *refs):
    others = refs[:8]
    if with_encodings:
        encs, grads = refs[8:16], refs[16]
        outs, turned, total = refs[17:21], refs[21], refs[22]
    else:
        outs, turned = refs[8:12], refs[12]
    tokens, width = rows.shape[1:]
    per = outs[0].shape[2]
    for r in range(8):
        turned[:, pl.ds(r * tokens, tokens)] = rows[r].T
    if with_encodings:
        length = encs[0].shape[1]
        sums = tn(grads[0], encs[0][...])
        for p in range(1, 8):
            sums += tn(grads[p], encs[p][...])
        total[pl.ds(0, length), :] = (sums * rescale).T
        total[pl.ds(length, 8), :] = jnp.zeros((8, total.shape[1]), F32)
    for i in range(SIDE):
        for j in range(SIDE):
            place = blocks[i * SIDE + j]
            lanes = pl.ds(pl.multiple_of(place * per, per), per)
            other = jnp.concatenate([ref[:, lanes] for ref in others], axis=0)
            term = jnp.dot(turned[...], other, preferred_element_type=F32) * rescale
            outs[i][j, :width] = term.astype(BF16)
            if with_encodings:
                at = pl.ds(pl.multiple_of(place * ENC_ROWS, 8), ENC_SLOT)
                outs[i][j, width : width + ENC_SLOT] = total[at, :width].astype(BF16)
                outs[i][j, width + ENC_SLOT :] = total[at, width:].astype(BF16)


ENC_ROWS = ENC_WIDTH // (SIDE * SIDE)
ENC_SLOT = 64


def weight_term(blocks, rows, others, rescale, name, encs=None, grads=None):
    count, tokens, width = rows.shape
    d = others[0].shape[1]
    per = d // (SIDE * SIDE)
    with_encodings = encs is not None
    height = width + 2 * ENC_SLOT if with_encodings else width
    whole = pl.BlockSpec(memory_space=pltpu.VMEM)
    scratch = [pltpu.VMEM((width, count * tokens), BF16)]
    operands = [rows, *others]
    flops = 2 * count * tokens * width * d
    if with_encodings:
        scratch += [pltpu.VMEM((ENC_WIDTH + 8, 2 * width), F32)]
        operands += [*encs, grads]
        flops += 2 * grads.size * ENC_WIDTH
    return pl.pallas_call(
        functools.partial(weight_kernel, rescale, with_encodings),
        in_specs=[pl.BlockSpec(memory_space=pltpu.SMEM)] + [whole] * len(operands),
        out_specs=[whole] * SIDE,
        scratch_shapes=scratch,
        out_shape=[jax.ShapeDtypeStruct((SIDE, height, per), BF16)] * SIDE,
        compiler_params=pltpu.CompilerParams(vmem_limit_bytes=(36 if with_encodings else 18) * MB),
        cost_estimate=pl.CostEstimate(
            flops=flops, bytes_accessed=2 * d * (count * tokens + width), transcendentals=0
        ),
        name=name,
    )(blocks, *operands)


def fetch_encodings(database, nbr_shard, nbr_row, x, y, core):
    requests = nbr_shard.shape[0] * NEIGHBOURS
    slice_len = database.shape[1]
    shard_flat = nbr_shard.reshape(requests)
    row_flat = nbr_row.reshape(requests)
    mine = jnp.stack([shard_flat, row_flat]).astype(jnp.int32)
    line = jnp.stack([mine] + [along_x(mine, SIDE - i) for i in range(1, SIDE)])
    tables = jnp.stack([line] + [along_y(line, SIDE - j) for j in range(1, SIDE)], axis=1)
    me = x * SIDE + y
    wanted = tables[:, :, 0] == me
    order = jnp.arange(requests, dtype=jnp.int32)
    before = (order[None, :] < order[:, None]).astype(F32)
    slot = jnp.einsum("ijs,rs->ijr", wanted.astype(F32), before)
    slots = jnp.arange(CAPACITY, dtype=jnp.int32)
    chosen = wanted[:, :, None, :] & (
        slot[:, :, None, :].astype(jnp.int32) == slots[None, None, :, None]
    )
    rows = jnp.sum(jnp.where(chosen, tables[:, :, 1][:, :, None, :], 0), axis=3)
    rows = jnp.roll(rows, (x, y), axis=(0, 1))
    served = jnp.take(database, rows.reshape(-1), axis=0)
    came = lax.all_to_all(served, "db", split_axis=0, concat_axis=0, tiled=True)
    same = (shard_flat[:, None] == shard_flat[None, :]) & (order[None, :] < order[:, None])
    slot_index = jnp.sum(same.astype(jnp.int32), axis=1)
    picked = jnp.take(came, shard_flat * CAPACITY + slot_index, axis=0)
    return picked.reshape(requests * slice_len, ENC_WIDTH)


def per_device(hidden, grad_out, w_query, w_key, w_value, w_out, database, nbr_shard, nbr_row):
    db = lax.axis_index("db")
    seq = lax.axis_index("seq")
    x, y = db // SIDE, db % SIDE
    z, core = seq // CORES, seq % CORES
    spans = nbr_shard.shape[0]
    width = w_query.shape[1]
    token_rows = hidden.shape[0]
    total_tokens = token_rows * lax.axis_size("db") * lax.axis_size("seq")
    rescale = float(total_tokens) ** (-0.5)
    block = jnp.arange(CHIPS * CORES, dtype=jnp.int32)
    places = jnp.argmax(piece_blocks(z, core)[None, :] == block[:, None], axis=1).astype(jnp.int32)
    i, j = jnp.arange(SIDE)[:, None], jnp.arange(SIDE)[None, :]
    blocks = jnp.where(
        core == 0,
        ((x + i) % SIDE) * SIDE + (y + j) % SIDE,
        ((x + j) % SIDE) * SIDE + (y + i) % SIDE,
    )
    blocks = blocks.reshape(-1).astype(jnp.int32)

    hidden_low = along_z(hidden)
    hidden_high = along_z(hidden, -1)
    grad_low = along_z(grad_out)
    grad_high = along_z(grad_out, -1)
    hidden_far = along_z(hidden_low)
    encoded = fetch_encodings(database, nbr_shard, nbr_row, x, y, core)
    enc_low = along_z(after(encoded, hidden_low))
    enc_high = along_z(after(encoded, hidden_low), -1)
    grad_far = along_z(grad_low)
    enc_far = along_z(enc_low)
    hidden_all = arrange(hidden, hidden_low, hidden_high, hidden_far)
    grad_all = arrange(grad_out, grad_low, grad_high, grad_far)
    enc_all = arrange(encoded, enc_low, enc_high, enc_far)

    w_both = jnp.concatenate([w_query, other_core(after(w_query, hidden_far))], axis=1)
    query = jnp.stack(
        [jnp.dot(piece, w_query, preferred_element_type=F32).astype(BF16) for piece in hidden_all]
    )
    gctx = jnp.stack([nt(piece, w_out).astype(BF16) for piece in grad_all])
    w_kv = jnp.concatenate([w_key, w_value], axis=1)
    kv = [
        jnp.dot(piece, w_kv, preferred_element_type=F32).astype(BF16).reshape(spans, -1, 2 * width)
        for piece in enc_all
    ]
    context, grad_query, grad_kv = attention(places, query, gctx, kv)

    joined = jnp.concatenate([grad_query[:4], other_core(grad_query[4:])], axis=2)
    query_term = weight_term(blocks, grad_query, hidden_all, rescale, "query_term")
    joined = after(joined, query_term[0])
    far = nt(joined[1], w_both).astype(BF16)
    from_far = along_z(far)
    crossing = nt(joined[3], w_both).astype(BF16)
    from_other = along_z(crossing, flip=1)
    out_term = weight_term(
        blocks,
        after(context, far, crossing),
        grad_all,
        rescale,
        "out_term",
        enc_all,
        grad_kv.reshape(8, -1, 2 * width),
    )
    near = (nt(joined[2], w_both) + from_far.astype(F32)).astype(BF16)
    from_near = along_z(near)
    own = after(nt(joined[0], w_both), near)
    grad_hidden = (own + from_other.astype(F32) + from_near.astype(F32)).astype(BF16)

    grad_w_query = reduce_over_db(query_term).T
    rest = reduce_over_db(out_term)
    grad_w_out = rest[:width]
    grad_w_key = rest[width : width + ENC_ROWS]
    grad_w_value = rest[width + ENC_SLOT : width + ENC_SLOT + ENC_ROWS]
    return grad_hidden, grad_w_query, grad_w_key, grad_w_value, grad_w_out


def solution(mesh):
    return jax.shard_map(
        per_device,
        mesh=mesh,
        in_specs=(
            P(("db", "seq"), None),
            P(("db", "seq"), None),
            P(None, "seq"),
            P(None, "seq"),
            P(None, "seq"),
            P("seq", None),
            P("db", "seq", None),
            P("db", None),
            P("db", None),
        ),
        out_specs=(
            P(("db", "seq"), None),
            P("db", "seq"),
            P("db", "seq"),
            P("db", "seq"),
            P("seq", "db"),
        ),
        check_vma=False,
    )
```

```python
import functools

import jax
import jax.numpy as jnp
from jax import lax
from jax.experimental import pallas as pl
from jax.experimental.pallas import tpu as pltpu
from jax.sharding import PartitionSpec as P

HEAD_SIZE = 128
ENC_WIDTH = 896
SPAN_LEN = 64
NEIGHBOURS = 2
CAPACITY = 3
SIDE = 4
CHIPS = 4
CORES = 2
MB = 1 << 20
F32 = jnp.float32
BF16 = jnp.bfloat16


def line_pairs(step):
    def pairs(phase):
        out = []
        for x in range(SIDE):
            for y in range(SIDE):
                for z in range(CHIPS):
                    for c in range(CORES):
                        dx, dy = (step, 0) if c == phase else (0, step)
                        there = ((x + dx) % SIDE) * SIDE + (y + dy) % SIDE
                        seq = z * CORES + c
                        out.append(((x * SIDE + y) * CHIPS * CORES + seq, there * CHIPS * CORES + seq))
        return out

    return pairs


def spread(array, step, phase):
    return lax.ppermute(array, ("db", "seq"), line_pairs(step)(phase))


def along_x(array, step):
    pairs = [
        (x * SIDE + y, ((x + step) % SIDE) * SIDE + y) for x in range(SIDE) for y in range(SIDE)
    ]
    return lax.ppermute(array, "db", pairs)


def along_y(array, step):
    pairs = [
        (x * SIDE + y, x * SIDE + (y + step) % SIDE) for x in range(SIDE) for y in range(SIDE)
    ]
    return lax.ppermute(array, "db", pairs)


def along_z(array, way=1):
    pairs = [
        (z * CORES + c, ((z + way * (1 - 2 * c)) % CHIPS) * CORES + c)
        for z in range(CHIPS)
        for c in range(CORES)
    ]
    return lax.ppermute(array, "seq", pairs)


def other_core(array):
    pairs = [(z * CORES + c, z * CORES + 1 - c) for z in range(CHIPS) for c in range(CORES)]
    return lax.ppermute(array, "seq", pairs)


def after(array, *others):
    return lax.optimization_barrier((array, others))[0]


def piece_blocks(z, core):
    s = 1 - 2 * core
    chips = jnp.stack([0 * s, 0 * s + 2, s, -s, 0 * s, 0 * s + 2, -s, s])
    cores = jnp.stack([core] * 4 + [1 - core] * 4)
    return ((z + chips) % CHIPS) * CORES + cores


def reduce_lines(terms, phase):
    total = terms[0].astype(F32)
    for i in range(1, SIDE):
        total = total + spread(terms[i], i, phase).astype(F32)
    return total


def nt(a, b):
    return lax.dot_general(a, b, (((1,), (1,)), ((), ())), preferred_element_type=F32)


def tn(a, b):
    return lax.dot_general(a, b, (((0,), (0,)), ((), ())), preferred_element_type=F32)


def attention_kernel(places, query, gctx, *refs):
    kv = refs[:8]
    ctx_out, gq_out, gkv_out = refs[8:11]
    q_s, g_s, c_s, gq_s = refs[11:]
    scale = HEAD_SIZE ** (-0.5)
    rows = query.shape[1]
    count = query.shape[0]
    width = query.shape[2]
    heads = width // HEAD_SIZE
    spans = kv[0].shape[0]
    part = kv[0].shape[1]
    total = count * rows
    for p in range(count):
        r = places[p]
        q_s[pl.ds(1 + p * rows, rows), :] = query[r].astype(F32)
        g_s[pl.ds(1 + p * rows, rows), :] = gctx[r].astype(F32)
    q_s[pl.ds(total + 1, SPAN_LEN - 1), :] = jnp.zeros((SPAN_LEN - 1, width), F32)
    g_s[pl.ds(total + 1, SPAN_LEN - 1), :] = jnp.zeros((SPAN_LEN - 1, width), F32)
    c_s[pl.ds(0, SPAN_LEN), :] = jnp.zeros((SPAN_LEN, width), F32)
    gq_s[pl.ds(0, SPAN_LEN), :] = jnp.zeros((SPAN_LEN, width), F32)

    def span(c, carry):
        at = pl.ds(pl.multiple_of((c + 1) * SPAN_LEN, SPAN_LEN), SPAN_LEN)
        both = jnp.concatenate([ref[c] for ref in kv], axis=0)
        q = q_s[at, :].astype(BF16)
        g = g_s[at, :].astype(BF16)
        for h in range(heads):
            lanes = slice(h * HEAD_SIZE, (h + 1) * HEAD_SIZE)
            vlanes = slice(width + h * HEAD_SIZE, width + (h + 1) * HEAD_SIZE)
            qh, gh, k, v = q[:, lanes], g[:, lanes], both[:, lanes], both[:, vlanes]
            expo = jnp.exp(nt(qh, k) * scale)
            probs = expo * (1.0 / jnp.sum(expo, axis=-1, keepdims=True))
            low = probs.astype(BF16)
            c_s[at, lanes] = jnp.dot(low, v, preferred_element_type=F32)
            gp = nt(gh, v)
            inner = jnp.sum(probs * gp, axis=-1, keepdims=True)
            gs = (probs * (gp - inner) * scale).astype(BF16)
            gq_s[at, lanes] = jnp.dot(gs, k, preferred_element_type=F32)
            gk = tn(gs, qh).astype(BF16)
            gv = tn(low, gh).astype(BF16)
            for p in range(8):
                gkv_out[p, c, :, lanes] = gk[p * part : (p + 1) * part]
                gkv_out[p, c, :, vlanes] = gv[p * part : (p + 1) * part]
        return carry

    lax.fori_loop(0, spans, span, 0, unroll=4)
    for p in range(count):
        r = places[p]
        ctx_out[r] = c_s[pl.ds(1 + p * rows, rows), :].astype(BF16)
        gq_out[r] = gq_s[pl.ds(1 + p * rows, rows), :].astype(BF16)


def attention(places, query, gctx, kv):
    count, rows, width = query.shape
    total = count * rows
    spans, part, both = kv[0].shape
    vmem = pl.BlockSpec(memory_space=pltpu.VMEM)
    scratch = pltpu.VMEM((total + SPAN_LEN, width), F32)
    flops = 14 * total * both // 2 * 256
    return pl.pallas_call(
        attention_kernel,
        out_shape=(
            jax.ShapeDtypeStruct((count, rows, width), BF16),
            jax.ShapeDtypeStruct((count, rows, width), BF16),
            jax.ShapeDtypeStruct((8, spans, part, both), BF16),
        ),
        in_specs=[pl.BlockSpec(memory_space=pltpu.SMEM)] + [vmem] * 10,
        out_specs=(vmem, vmem, vmem),
        scratch_shapes=[scratch] * 4,
        compiler_params=pltpu.CompilerParams(vmem_limit_bytes=16 * MB),
        cost_estimate=pl.CostEstimate(
            flops=flops, bytes_accessed=10 * MB, transcendentals=spans * 64 * 512
        ),
        name="attention",
    )(places, query, gctx, *kv)


def weight_kernel(rescale, with_encodings, blocks, rows, *refs):
    others = refs[:2]
    if with_encodings:
        encs, grads = refs[2:10], refs[10]
        outs, turned, total = refs[11:15], refs[15], refs[16]
    else:
        outs, turned = refs[2:6], refs[6]
    tokens, width = rows.shape[1:]
    per = outs[0].shape[2]
    for r in range(8):
        turned[:, pl.ds(r * tokens, tokens)] = rows[r].T
    if with_encodings:
        length = encs[0].shape[1]
        sums = tn(grads[0], encs[0][...])
        for p in range(1, 8):
            sums += tn(grads[p], encs[p][...])
        total[pl.ds(0, length), :] = (sums * rescale).T
        total[pl.ds(length, 8), :] = jnp.zeros((8, total.shape[1]), F32)
    for i in range(SIDE):
        places = [blocks[i * SIDE + j] for j in range(SIDE)]
        lanes = [pl.ds(pl.multiple_of(place * per, per), per) for place in places]
        other = jnp.concatenate(
            [jnp.concatenate([ref[:, at] for ref in others], axis=0) for at in lanes], axis=1
        )
        term = jnp.dot(turned[...], other, preferred_element_type=F32) * rescale
        for j in range(SIDE):
            outs[i][j, :width] = term[:, j * per : (j + 1) * per].astype(BF16)
            if with_encodings:
                at = pl.ds(pl.multiple_of(places[j] * ENC_ROWS, 8), ENC_SLOT)
                outs[i][j, width : width + ENC_SLOT] = total[at, :width].astype(BF16)
                outs[i][j, width + ENC_SLOT :] = total[at, width:].astype(BF16)


ENC_ROWS = ENC_WIDTH // (SIDE * SIDE)
ENC_SLOT = 64


def weight_term(blocks, rows, others, rescale, name, encs=None, grads=None):
    count, tokens, width = rows.shape
    d = others[0].shape[1]
    per = d // (SIDE * SIDE)
    with_encodings = encs is not None
    height = width + 2 * ENC_SLOT if with_encodings else width
    whole = pl.BlockSpec(memory_space=pltpu.VMEM)
    scratch = [pltpu.VMEM((width, count * tokens), BF16)]
    operands = [rows, *others]
    flops = 2 * count * tokens * width * d
    if with_encodings:
        scratch += [pltpu.VMEM((ENC_WIDTH + 8, 2 * width), F32)]
        operands += [*encs, grads]
        flops += 2 * grads.size * ENC_WIDTH
    return pl.pallas_call(
        functools.partial(weight_kernel, rescale, with_encodings),
        in_specs=[pl.BlockSpec(memory_space=pltpu.SMEM)] + [whole] * len(operands),
        out_specs=[whole] * SIDE,
        scratch_shapes=scratch,
        out_shape=[jax.ShapeDtypeStruct((SIDE, height, per), BF16)] * SIDE,
        compiler_params=pltpu.CompilerParams(vmem_limit_bytes=(36 if with_encodings else 18) * MB),
        cost_estimate=pl.CostEstimate(
            flops=flops, bytes_accessed=2 * d * (count * tokens + width), transcendentals=0
        ),
        name=name,
    )(blocks, *operands)


def request_tables(nbr_shard, nbr_row):
    mine = jnp.stack([nbr_shard.reshape(-1), nbr_row.reshape(-1)]).astype(jnp.int32)
    line = jnp.stack([mine] + [along_x(mine, SIDE - i) for i in range(1, SIDE)])
    return jnp.stack([line] + [along_y(line, SIDE - j) for j in range(1, SIDE)], axis=1)


def take_rows(array, index):
    return array.at[index].get(mode="promise_in_bounds")


def fetch_encodings(tables, database, nbr_shard, x, y):
    requests = nbr_shard.shape[0] * NEIGHBOURS
    slice_len = database.shape[1]
    shard_flat = nbr_shard.reshape(requests)
    me = x * SIDE + y
    wanted = tables[:, :, 0] == me
    order = jnp.arange(requests, dtype=jnp.int32)
    before = (order[None, :] < order[:, None]).astype(F32)
    slot = jnp.einsum("ijs,rs->ijr", wanted.astype(F32), before)
    slots = jnp.arange(CAPACITY, dtype=jnp.int32)
    chosen = wanted[:, :, None, :] & (
        slot[:, :, None, :].astype(jnp.int32) == slots[None, None, :, None]
    )
    rows = jnp.sum(jnp.where(chosen, tables[:, :, 1][:, :, None, :], 0), axis=3)
    rows = jnp.roll(rows, (x, y), axis=(0, 1))
    served = take_rows(database, rows.reshape(-1))
    came = lax.all_to_all(served, "db", split_axis=0, concat_axis=0, tiled=True)
    same = (shard_flat[:, None] == shard_flat[None, :]) & (order[None, :] < order[:, None])
    slot_index = jnp.sum(same.astype(jnp.int32), axis=1)
    picked = take_rows(came, shard_flat * CAPACITY + slot_index)
    return picked.reshape(requests * slice_len, ENC_WIDTH)


def per_device(hidden, grad_out, w_query, w_key, w_value, w_out, database, nbr_shard, nbr_row):
    db = lax.axis_index("db")
    seq = lax.axis_index("seq")
    x, y = db // SIDE, db % SIDE
    z, core = seq // CORES, seq % CORES
    spans = nbr_shard.shape[0]
    width = w_query.shape[1]
    token_rows = hidden.shape[0]
    total_tokens = token_rows * lax.axis_size("db") * lax.axis_size("seq")
    rescale = float(total_tokens) ** (-0.5)
    block = jnp.arange(CHIPS * CORES, dtype=jnp.int32)
    places = jnp.argmax(piece_blocks(z, core)[None, :] == block[:, None], axis=1).astype(jnp.int32)
    i, j = jnp.arange(SIDE)[:, None], jnp.arange(SIDE)[None, :]
    blocks = jnp.where(
        core == 0,
        ((x + i) % SIDE) * SIDE + (y + j) % SIDE,
        ((x + j) % SIDE) * SIDE + (y + i) % SIDE,
    )
    blocks = blocks.reshape(-1).astype(jnp.int32)

    tables = request_tables(nbr_shard, nbr_row)
    hidden_low = along_z(hidden)
    hidden_high = along_z(hidden, -1)
    grad_rows = after(grad_out, tables)
    grad_low = along_z(grad_rows)
    grad_high = along_z(grad_rows, -1)
    hidden_far = along_z(hidden_low)
    encoded = fetch_encodings(tables, database, nbr_shard, x, y)
    grad_far = along_z(grad_low)
    enc_rows = after(encoded, hidden_high, grad_high)
    enc_low = along_z(enc_rows)
    enc_high = along_z(enc_rows, -1)
    hidden_far = after(hidden_far, encoded)
    hidden_own = jnp.concatenate([hidden, hidden_far, hidden_high, hidden_low], axis=0)
    hidden_all = [hidden_own, other_core(hidden_own)]
    grad_own = jnp.concatenate([grad_out, grad_far, grad_high, grad_low], axis=0)
    grad_all = [grad_own, other_core(grad_own)]
    w_both = jnp.concatenate([w_query, other_core(after(w_query, hidden_far))], axis=1)

    pieces = 2 * CHIPS
    query = jnp.concatenate(
        [jnp.dot(rows, w_query, preferred_element_type=F32).astype(BF16) for rows in hidden_all]
    ).reshape(pieces, token_rows, width)
    gctx = jnp.concatenate([nt(rows, w_out).astype(BF16) for rows in grad_all])
    gctx = gctx.reshape(pieces, token_rows, width)
    enc_far = along_z(after(enc_low, query, gctx))
    enc_all = [encoded, enc_far, enc_high, enc_low]
    enc_all += [other_core(piece) for piece in enc_all]
    w_kv = jnp.concatenate([w_key, w_value], axis=1)
    kv = [
        jnp.dot(piece, w_kv, preferred_element_type=F32).astype(BF16).reshape(spans, -1, 2 * width)
        for piece in enc_all
    ]
    context, grad_query, grad_kv = attention(places, query, gctx, kv)

    joined = jnp.concatenate([grad_query[:4], other_core(grad_query[4:])], axis=2)
    out_term = weight_term(blocks, context, grad_all, rescale, "out_term")
    joined = after(joined, out_term[0])
    far = nt(joined[1], w_both).astype(BF16)
    from_far = along_z(far)
    back = nt(joined[3], w_both).astype(BF16)
    from_back = along_z(back, -1)
    query_term = weight_term(
        blocks,
        after(grad_query, far, back),
        hidden_all,
        rescale,
        "query_term",
        enc_all,
        grad_kv.reshape(8, -1, 2 * width),
    )
    near = (nt(joined[2], w_both) + after(from_far, from_back).astype(F32)).astype(BF16)
    from_near = along_z(near)
    own = after(nt(joined[0], w_both) + from_back.astype(F32), near)
    grad_hidden = (own + from_near.astype(F32)).astype(BF16)

    totals = [reduce_lines(out_term, 0).astype(BF16), reduce_lines(query_term, 0).astype(BF16)]
    rest = reduce_lines(list(jnp.concatenate(totals, axis=1)), 1)
    grad_w_out, grad_w_query, rest = rest[:width], rest[width : 2 * width].T, rest[2 * width :]
    grad_w_key, grad_w_value = rest[:ENC_ROWS], rest[ENC_SLOT : ENC_SLOT + ENC_ROWS]
    return grad_hidden, grad_w_query, grad_w_key, grad_w_value, grad_w_out


def solution(mesh):
    return jax.shard_map(
        per_device,
        mesh=mesh,
        in_specs=(
            P(("db", "seq"), None),
            P(("db", "seq"), None),
            P(None, "seq"),
            P(None, "seq"),
            P(None, "seq"),
            P("seq", None),
            P("db", "seq", None),
            P("db", None),
            P("db", None),
        ),
        out_specs=(
            P(("db", "seq"), None),
            P("db", "seq"),
            P("db", "seq"),
            P("db", "seq"),
            P("seq", "db"),
        ),
        check_vma=False,
    )
```

```python
import functools

import jax
import jax.numpy as jnp
from jax import lax
from jax.experimental import pallas as pl
from jax.experimental.pallas import tpu as pltpu
from jax.sharding import PartitionSpec as P

HEAD_SIZE = 128
ENC_WIDTH = 896
SPAN_LEN = 64
NEIGHBOURS = 2
CAPACITY = 3
SIDE = 4
CHIPS = 4
CORES = 2
MB = 1 << 20
F32 = jnp.float32
BF16 = jnp.bfloat16


def line_pairs(step):
    def pairs(phase):
        out = []
        for x in range(SIDE):
            for y in range(SIDE):
                for z in range(CHIPS):
                    for c in range(CORES):
                        dx, dy = (step, 0) if c == phase else (0, step)
                        there = ((x + dx) % SIDE) * SIDE + (y + dy) % SIDE
                        seq = z * CORES + c
                        out.append(((x * SIDE + y) * CHIPS * CORES + seq, there * CHIPS * CORES + seq))
        return out

    return pairs


def spread(array, step, phase):
    return lax.ppermute(array, ("db", "seq"), line_pairs(step)(phase))


def along_x(array, step):
    pairs = [
        (x * SIDE + y, ((x + step) % SIDE) * SIDE + y) for x in range(SIDE) for y in range(SIDE)
    ]
    return lax.ppermute(array, "db", pairs)


def along_y(array, step):
    pairs = [
        (x * SIDE + y, x * SIDE + (y + step) % SIDE) for x in range(SIDE) for y in range(SIDE)
    ]
    return lax.ppermute(array, "db", pairs)


def along_z(array, way=1):
    pairs = [
        (z * CORES + c, ((z + way * (1 - 2 * c)) % CHIPS) * CORES + c)
        for z in range(CHIPS)
        for c in range(CORES)
    ]
    return lax.ppermute(array, "seq", pairs)


def other_core(array):
    pairs = [(z * CORES + c, z * CORES + 1 - c) for z in range(CHIPS) for c in range(CORES)]
    return lax.ppermute(array, "seq", pairs)


def after(array, *others):
    return lax.optimization_barrier((array, others))[0]


def piece_blocks(z, core):
    s = 1 - 2 * core
    chips = jnp.stack([0 * s, 0 * s + 2, s, -s, 0 * s, 0 * s + 2, -s, s])
    cores = jnp.stack([core] * 4 + [1 - core] * 4)
    return ((z + chips) % CHIPS) * CORES + cores


def reduce_lines(terms, phase):
    total = terms[0].astype(F32)
    for i in range(1, SIDE):
        total = total + spread(terms[i], i, phase).astype(F32)
    return total


def nt(a, b):
    return lax.dot_general(a, b, (((1,), (1,)), ((), ())), preferred_element_type=F32)


def tn(a, b):
    return lax.dot_general(a, b, (((0,), (0,)), ((), ())), preferred_element_type=F32)


def attention_kernel(places, query, gctx, *refs):
    kv = refs[:8]
    ctx_out, gq_out, gkv_out = refs[8:11]
    q_s, g_s, c_s, gq_s = refs[11:]
    scale = HEAD_SIZE ** (-0.5)
    rows = query.shape[1]
    count = query.shape[0]
    width = query.shape[2]
    heads = width // HEAD_SIZE
    spans = kv[0].shape[0]
    part = kv[0].shape[1]
    total = count * rows
    for p in range(count):
        r = places[p]
        q_s[pl.ds(1 + p * rows, rows), :] = query[r].astype(F32)
        g_s[pl.ds(1 + p * rows, rows), :] = gctx[r].astype(F32)
    q_s[pl.ds(total + 1, SPAN_LEN - 1), :] = jnp.zeros((SPAN_LEN - 1, width), F32)
    g_s[pl.ds(total + 1, SPAN_LEN - 1), :] = jnp.zeros((SPAN_LEN - 1, width), F32)
    c_s[pl.ds(0, SPAN_LEN), :] = jnp.zeros((SPAN_LEN, width), F32)
    gq_s[pl.ds(0, SPAN_LEN), :] = jnp.zeros((SPAN_LEN, width), F32)

    def stacked(rows_in):
        lane = lax.broadcasted_iota(jnp.int32, rows_in.shape, 1) // HEAD_SIZE
        parts = [jnp.where(lane == h, rows_in, 0.0) for h in range(heads)]
        return jnp.concatenate(parts, axis=0).astype(BF16)

    def span(c, carry):
        at = pl.ds(pl.multiple_of((c + 1) * SPAN_LEN, SPAN_LEN), SPAN_LEN)
        both = jnp.concatenate([ref[c] for ref in kv], axis=0)
        k, v = both[:, :width], both[:, width:]
        q = stacked(q_s[at, :])
        g = stacked(g_s[at, :])
        expo = jnp.exp(nt(k, q) * scale)
        probs = expo * (1.0 / jnp.sum(expo, axis=0, keepdims=True))
        low = probs.astype(BF16)
        gp = nt(v, g)
        inner = jnp.sum(probs * gp, axis=0, keepdims=True)
        gs = (probs * (gp - inner) * scale).astype(BF16)
        low_t, gs_t = low.T, gs.T
        for h in range(heads):
            lanes = slice(h * HEAD_SIZE, (h + 1) * HEAD_SIZE)
            tokens = slice(h * SPAN_LEN, (h + 1) * SPAN_LEN)
            c_s[at, lanes] = jnp.dot(low_t[tokens], v[:, lanes], preferred_element_type=F32)
            gq_s[at, lanes] = jnp.dot(gs_t[tokens], k[:, lanes], preferred_element_type=F32)
        gk = jnp.dot(gs, q, preferred_element_type=F32).astype(BF16)
        gv = jnp.dot(low, g, preferred_element_type=F32).astype(BF16)
        for p in range(8):
            gkv_out[p, c, :, :width] = gk[p * part : (p + 1) * part]
            gkv_out[p, c, :, width:] = gv[p * part : (p + 1) * part]
        return carry

    lax.fori_loop(0, spans, span, 0, unroll=True)
    for p in range(count):
        r = places[p]
        ctx_out[r] = c_s[pl.ds(1 + p * rows, rows), :].astype(BF16)
        gq_out[r] = gq_s[pl.ds(1 + p * rows, rows), :].astype(BF16)


def attention(places, query, gctx, kv):
    count, rows, width = query.shape
    total = count * rows
    spans, part, both = kv[0].shape
    vmem = pl.BlockSpec(memory_space=pltpu.VMEM)
    scratch = pltpu.VMEM((total + SPAN_LEN, width), F32)
    flops = 14 * total * both // 2 * 256
    return pl.pallas_call(
        attention_kernel,
        out_shape=(
            jax.ShapeDtypeStruct((count, rows, width), BF16),
            jax.ShapeDtypeStruct((count, rows, width), BF16),
            jax.ShapeDtypeStruct((8, spans, part, both), BF16),
        ),
        in_specs=[pl.BlockSpec(memory_space=pltpu.SMEM)] + [vmem] * 10,
        out_specs=(vmem, vmem, vmem),
        scratch_shapes=[scratch] * 4,
        compiler_params=pltpu.CompilerParams(vmem_limit_bytes=16 * MB),
        cost_estimate=pl.CostEstimate(
            flops=flops, bytes_accessed=10 * MB, transcendentals=spans * 64 * 512
        ),
        name="attention",
    )(places, query, gctx, *kv)


def weight_kernel(rescale, with_encodings, blocks, rows, *refs):
    others = refs[:2]
    if with_encodings:
        encs, grads = refs[2:10], refs[10]
        outs, turned, total = refs[11:15], refs[15], refs[16]
    else:
        outs, turned = refs[2:6], refs[6]
    tokens, width = rows.shape[1:]
    per = outs[0].shape[2]
    for r in range(8):
        turned[:, pl.ds(r * tokens, tokens)] = rows[r].T
    if with_encodings:
        length = encs[0].shape[1]
        sums = tn(encs[0][...], grads[0])
        for p in range(1, 8):
            sums += tn(encs[p][...], grads[p])
        total[pl.ds(0, length), :] = sums * rescale
        total[pl.ds(length, 8), :] = jnp.zeros((8, total.shape[1]), F32)
    for i in range(SIDE):
        places = [blocks[i * SIDE + j] for j in range(SIDE)]
        lanes = [pl.ds(pl.multiple_of(place * per, per), per) for place in places]
        other = jnp.concatenate(
            [jnp.concatenate([ref[:, at] for ref in others], axis=0) for at in lanes], axis=1
        )
        term = jnp.dot(turned[...], other, preferred_element_type=F32) * rescale
        for j in range(SIDE):
            outs[i][j, :width] = term[:, j * per : (j + 1) * per].astype(BF16)
            if with_encodings:
                at = pl.ds(pl.multiple_of(places[j] * ENC_ROWS, 8), ENC_SLOT)
                outs[i][j, width : width + ENC_SLOT] = total[at, :width].astype(BF16)
                outs[i][j, width + ENC_SLOT :] = total[at, width:].astype(BF16)


ENC_ROWS = ENC_WIDTH // (SIDE * SIDE)
ENC_SLOT = 64


def weight_term(blocks, rows, others, rescale, name, encs=None, grads=None):
    count, tokens, width = rows.shape
    d = others[0].shape[1]
    per = d // (SIDE * SIDE)
    with_encodings = encs is not None
    height = width + 2 * ENC_SLOT if with_encodings else width
    whole = pl.BlockSpec(memory_space=pltpu.VMEM)
    scratch = [pltpu.VMEM((width, count * tokens), BF16)]
    operands = [rows, *others]
    flops = 2 * count * tokens * width * d
    if with_encodings:
        scratch += [pltpu.VMEM((ENC_WIDTH + 8, 2 * width), F32)]
        operands += [*encs, grads]
        flops += 2 * grads.size * ENC_WIDTH
    return pl.pallas_call(
        functools.partial(weight_kernel, rescale, with_encodings),
        in_specs=[pl.BlockSpec(memory_space=pltpu.SMEM)] + [whole] * len(operands),
        out_specs=[whole] * SIDE,
        scratch_shapes=scratch,
        out_shape=[jax.ShapeDtypeStruct((SIDE, height, per), BF16)] * SIDE,
        compiler_params=pltpu.CompilerParams(vmem_limit_bytes=(20 if with_encodings else 10) * MB),
        cost_estimate=pl.CostEstimate(
            flops=flops, bytes_accessed=2 * d * (count * tokens + width), transcendentals=0
        ),
        name=name,
    )(blocks, *operands)


def request_tables(nbr_shard, nbr_row):
    mine = jnp.stack([nbr_shard.reshape(-1), nbr_row.reshape(-1)]).astype(jnp.int32)
    line = jnp.stack([mine] + [along_x(mine, SIDE - i) for i in range(1, SIDE)])
    return jnp.stack([line] + [along_y(line, SIDE - j) for j in range(1, SIDE)], axis=1)


def take_rows(array, index):
    return array.at[index].get(mode="promise_in_bounds")


def fetch_encodings(tables, database, nbr_shard, x, y):
    requests = nbr_shard.shape[0] * NEIGHBOURS
    slice_len = database.shape[1]
    shard_flat = nbr_shard.reshape(requests)
    me = x * SIDE + y
    wanted = tables[:, :, 0] == me
    order = jnp.arange(requests, dtype=jnp.int32)
    before = (order[None, :] < order[:, None]).astype(F32)
    slot = jnp.einsum("ijs,rs->ijr", wanted.astype(F32), before)
    slots = jnp.arange(CAPACITY, dtype=jnp.int32)
    chosen = wanted[:, :, None, :] & (
        slot[:, :, None, :].astype(jnp.int32) == slots[None, None, :, None]
    )
    rows = jnp.sum(jnp.where(chosen, tables[:, :, 1][:, :, None, :], 0), axis=3)
    rows = jnp.roll(rows, (x, y), axis=(0, 1))
    served = take_rows(database, rows.reshape(-1))
    came = lax.all_to_all(served, "db", split_axis=0, concat_axis=0, tiled=True)
    same = (shard_flat[:, None] == shard_flat[None, :]) & (order[None, :] < order[:, None])
    slot_index = jnp.sum(same.astype(jnp.int32), axis=1)
    picked = take_rows(came, shard_flat * CAPACITY + slot_index)
    return picked.reshape(requests * slice_len, ENC_WIDTH)


def per_device(hidden, grad_out, w_query, w_key, w_value, w_out, database, nbr_shard, nbr_row):
    db = lax.axis_index("db")
    seq = lax.axis_index("seq")
    x, y = db // SIDE, db % SIDE
    z, core = seq // CORES, seq % CORES
    spans = nbr_shard.shape[0]
    width = w_query.shape[1]
    token_rows = hidden.shape[0]
    total_tokens = token_rows * lax.axis_size("db") * lax.axis_size("seq")
    rescale = float(total_tokens) ** (-0.5)
    block = jnp.arange(CHIPS * CORES, dtype=jnp.int32)
    places = jnp.argmax(piece_blocks(z, core)[None, :] == block[:, None], axis=1).astype(jnp.int32)
    i, j = jnp.arange(SIDE)[:, None], jnp.arange(SIDE)[None, :]
    blocks = jnp.where(
        core == 0,
        ((x + i) % SIDE) * SIDE + (y + j) % SIDE,
        ((x + j) % SIDE) * SIDE + (y + i) % SIDE,
    )
    blocks = blocks.reshape(-1).astype(jnp.int32)

    tables = request_tables(nbr_shard, nbr_row)
    hidden_low = along_z(hidden)
    hidden_high = along_z(hidden, -1)
    grad_rows = after(grad_out, tables)
    grad_low = along_z(grad_rows)
    grad_high = along_z(grad_rows, -1)
    hidden_far = along_z(hidden_low)
    encoded = fetch_encodings(tables, database, nbr_shard, x, y)
    grad_far = along_z(grad_low)
    enc_rows = after(encoded, hidden_high, grad_high)
    enc_low = along_z(enc_rows)
    enc_high = along_z(enc_rows, -1)
    hidden_far = after(hidden_far, encoded)
    hidden_own = jnp.concatenate([hidden, hidden_far, hidden_high, hidden_low], axis=0)
    hidden_all = [hidden_own, other_core(hidden_own)]
    grad_own = jnp.concatenate([grad_out, grad_far, grad_high, grad_low], axis=0)
    grad_all = [grad_own, other_core(grad_own)]
    w_both = jnp.concatenate([w_query, other_core(after(w_query, hidden_far))], axis=1)

    pieces = 2 * CHIPS
    w_late, grad_late = after((w_query, w_out), enc_low)
    query = jnp.concatenate(
        [jnp.dot(rows, w_late, preferred_element_type=F32).astype(BF16) for rows in hidden_all]
    ).reshape(pieces, token_rows, width)
    gctx = jnp.concatenate([nt(rows, grad_late).astype(BF16) for rows in grad_all])
    gctx = gctx.reshape(pieces, token_rows, width)
    enc_far = along_z(enc_low)
    enc_all = [encoded, enc_far, enc_high, enc_low]
    enc_all += [other_core(piece) for piece in enc_all]
    w_kv = jnp.concatenate([w_key, w_value], axis=1)
    kv = [
        jnp.dot(piece, w_kv, preferred_element_type=F32).astype(BF16).reshape(spans, -1, 2 * width)
        for piece in enc_all
    ]
    context, grad_query, grad_kv = attention(places, query, gctx, kv)

    joined = jnp.concatenate([grad_query[:4], other_core(grad_query[4:])], axis=2)
    query_term = weight_term(blocks, grad_query, hidden_all, rescale, "query_term")
    joined = after(joined, query_term[0])
    far = nt(joined[1], w_both).astype(BF16)
    from_far = along_z(far)
    back = nt(joined[3], w_both).astype(BF16)
    from_back = along_z(back, -1)
    out_term = weight_term(
        blocks,
        after(context, far, back),
        grad_all,
        rescale,
        "out_term",
        enc_all,
        grad_kv.reshape(8, -1, 2 * width),
    )
    near = (nt(joined[2], w_both) + from_far.astype(F32)).astype(BF16)
    from_near = along_z(near)
    out_term = list(after(tuple(out_term), near))
    own = after(nt(joined[0], w_both) + from_back.astype(F32), near)
    grad_hidden = (own + from_near.astype(F32)).astype(BF16)

    totals = [reduce_lines(query_term, 0).astype(BF16), reduce_lines(out_term, 0).astype(BF16)]
    rest = reduce_lines(list(jnp.concatenate(totals, axis=1)), 1)
    grad_w_query, grad_w_out, rest = rest[:width].T, rest[width : 2 * width], rest[2 * width :]
    grad_w_key, grad_w_value = rest[:ENC_ROWS], rest[ENC_SLOT : ENC_SLOT + ENC_ROWS]
    return grad_hidden, grad_w_query, grad_w_key, grad_w_value, grad_w_out


def solution(mesh):
    return jax.shard_map(
        per_device,
        mesh=mesh,
        in_specs=(
            P(("db", "seq"), None),
            P(("db", "seq"), None),
            P(None, "seq"),
            P(None, "seq"),
            P(None, "seq"),
            P("seq", None),
            P("db", "seq", None),
            P("db", None),
            P("db", None),
        ),
        out_specs=(
            P(("db", "seq"), None),
            P("db", "seq"),
            P("db", "seq"),
            P("db", "seq"),
            P("seq", "db"),
        ),
        check_vma=False,
    )
```

```python
import functools

import jax
import jax.numpy as jnp
from jax import lax
from jax.experimental import pallas as pl
from jax.experimental.pallas import tpu as pltpu
from jax.sharding import PartitionSpec as P

HEAD_SIZE = 128
ENC_WIDTH = 896
SPAN_LEN = 64
NEIGHBOURS = 2
CAPACITY = 3
SIDE = 4
CHIPS = 4
CORES = 2
MB = 1 << 20
F32 = jnp.float32
BF16 = jnp.bfloat16


def line_pairs(step):
    def pairs(phase):
        out = []
        for x in range(SIDE):
            for y in range(SIDE):
                for z in range(CHIPS):
                    for c in range(CORES):
                        dx, dy = (step, 0) if c == phase else (0, step)
                        there = ((x + dx) % SIDE) * SIDE + (y + dy) % SIDE
                        seq = z * CORES + c
                        out.append(((x * SIDE + y) * CHIPS * CORES + seq, there * CHIPS * CORES + seq))
        return out

    return pairs


def spread(array, step, phase):
    return lax.ppermute(array, ("db", "seq"), line_pairs(step)(phase))


def along_x(array, step):
    pairs = [
        (x * SIDE + y, ((x + step) % SIDE) * SIDE + y) for x in range(SIDE) for y in range(SIDE)
    ]
    return lax.ppermute(array, "db", pairs)


def along_y(array, step):
    pairs = [
        (x * SIDE + y, x * SIDE + (y + step) % SIDE) for x in range(SIDE) for y in range(SIDE)
    ]
    return lax.ppermute(array, "db", pairs)


def along_z(array, way=1):
    pairs = [
        (z * CORES + c, ((z + way * (1 - 2 * c)) % CHIPS) * CORES + c)
        for z in range(CHIPS)
        for c in range(CORES)
    ]
    return lax.ppermute(array, "seq", pairs)


def other_core(array):
    pairs = [(z * CORES + c, z * CORES + 1 - c) for z in range(CHIPS) for c in range(CORES)]
    return lax.ppermute(array, "seq", pairs)


def after(array, *others):
    return lax.optimization_barrier((array, others))[0]


def piece_blocks(z, core):
    s = 1 - 2 * core
    chips = jnp.stack([0 * s, 0 * s + 2, s, -s, 0 * s, 0 * s + 2, -s, s])
    cores = jnp.stack([core] * 4 + [1 - core] * 4)
    return ((z + chips) % CHIPS) * CORES + cores


def reduce_lines(terms, phase):
    total = terms[0].astype(F32)
    for i in range(1, SIDE):
        total = total + spread(terms[i], i, phase).astype(F32)
    return total


def nt(a, b):
    return lax.dot_general(a, b, (((1,), (1,)), ((), ())), preferred_element_type=F32)


def tn(a, b):
    return lax.dot_general(a, b, (((0,), (0,)), ((), ())), preferred_element_type=F32)


def attention_kernel(places, query, gctx, *refs):
    kv = refs[:8]
    ctx_out, gq_out, gkv_out = refs[8:11]
    q_s, g_s, c_s, gq_s = refs[11:]
    scale = HEAD_SIZE ** (-0.5)
    rows = query.shape[1]
    count = query.shape[0]
    width = query.shape[2]
    heads = width // HEAD_SIZE
    spans = kv[0].shape[0]
    part = kv[0].shape[1]
    total = count * rows
    for p in range(count):
        r = places[p]
        q_s[pl.ds(1 + p * rows, rows), :] = query[r].astype(F32)
        g_s[pl.ds(1 + p * rows, rows), :] = gctx[r].astype(F32)
    q_s[pl.ds(total + 1, SPAN_LEN - 1), :] = jnp.zeros((SPAN_LEN - 1, width), F32)
    g_s[pl.ds(total + 1, SPAN_LEN - 1), :] = jnp.zeros((SPAN_LEN - 1, width), F32)
    c_s[pl.ds(0, SPAN_LEN), :] = jnp.zeros((SPAN_LEN, width), F32)
    gq_s[pl.ds(0, SPAN_LEN), :] = jnp.zeros((SPAN_LEN, width), F32)

    def stacked(rows_in):
        lane = lax.broadcasted_iota(jnp.int32, rows_in.shape, 1) // HEAD_SIZE
        parts = [jnp.where(lane == h, rows_in, 0.0) for h in range(heads)]
        return jnp.concatenate(parts, axis=0).astype(BF16)

    def span(c, carry):
        at = pl.ds(pl.multiple_of((c + 1) * SPAN_LEN, SPAN_LEN), SPAN_LEN)
        both = jnp.concatenate([ref[c] for ref in kv], axis=0)
        k, v = both[:, :width], both[:, width:]
        q = stacked(q_s[at, :])
        g = stacked(g_s[at, :])
        expo = jnp.exp(nt(k, q) * scale)
        probs = expo * (1.0 / jnp.sum(expo, axis=0, keepdims=True))
        low = probs.astype(BF16)
        gp = nt(v, g)
        inner = jnp.sum(probs * gp, axis=0, keepdims=True)
        gs = (probs * (gp - inner) * scale).astype(BF16)
        low_t, gs_t = low.T, gs.T
        for h in range(heads):
            lanes = slice(h * HEAD_SIZE, (h + 1) * HEAD_SIZE)
            tokens = slice(h * SPAN_LEN, (h + 1) * SPAN_LEN)
            c_s[at, lanes] = jnp.dot(low_t[tokens], v[:, lanes], preferred_element_type=F32)
            gq_s[at, lanes] = jnp.dot(gs_t[tokens], k[:, lanes], preferred_element_type=F32)
        gk = jnp.dot(gs, q, preferred_element_type=F32).astype(BF16)
        gv = jnp.dot(low, g, preferred_element_type=F32).astype(BF16)
        for p in range(8):
            gkv_out[p, c, :, :width] = gk[p * part : (p + 1) * part]
            gkv_out[p, c, :, width:] = gv[p * part : (p + 1) * part]
        return carry

    lax.fori_loop(0, spans, span, 0, unroll=True)
    for p in range(count):
        r = places[p]
        ctx_out[r] = c_s[pl.ds(1 + p * rows, rows), :].astype(BF16)
        gq_out[r] = gq_s[pl.ds(1 + p * rows, rows), :].astype(BF16)


def attention(places, query, gctx, kv):
    count, rows, width = query.shape
    total = count * rows
    spans, part, both = kv[0].shape
    vmem = pl.BlockSpec(memory_space=pltpu.VMEM)
    scratch = pltpu.VMEM((total + SPAN_LEN, width), F32)
    flops = 14 * total * both // 2 * 256
    return pl.pallas_call(
        attention_kernel,
        out_shape=(
            jax.ShapeDtypeStruct((count, rows, width), BF16),
            jax.ShapeDtypeStruct((count, rows, width), BF16),
            jax.ShapeDtypeStruct((8, spans, part, both), BF16),
        ),
        in_specs=[pl.BlockSpec(memory_space=pltpu.SMEM)] + [vmem] * 10,
        out_specs=(vmem, vmem, vmem),
        scratch_shapes=[scratch] * 4,
        compiler_params=pltpu.CompilerParams(vmem_limit_bytes=16 * MB),
        cost_estimate=pl.CostEstimate(
            flops=flops, bytes_accessed=10 * MB, transcendentals=spans * 64 * 512
        ),
        name="attention",
    )(places, query, gctx, *kv)


def weight_kernel(rescale, with_encodings, blocks, rows, *refs):
    others = refs[:2]
    if with_encodings:
        encs, grads = refs[2:10], refs[10]
        outs, turned, total = refs[11:15], refs[15], refs[16]
    else:
        outs, turned = refs[2:6], refs[6]
    tokens, width = rows.shape[1:]
    per = outs[0].shape[2]
    for r in range(8):
        turned[:, pl.ds(r * tokens, tokens)] = rows[r].T
    if with_encodings:
        length = encs[0].shape[1]
        sums = tn(encs[0][...], grads[0])
        for p in range(1, 8):
            sums += tn(encs[p][...], grads[p])
        total[pl.ds(0, length), :] = sums * rescale
        total[pl.ds(length, 8), :] = jnp.zeros((8, total.shape[1]), F32)
    for i in range(SIDE):
        places = [blocks[i * SIDE + j] for j in range(SIDE)]
        lanes = [pl.ds(pl.multiple_of(place * per, per), per) for place in places]
        other = jnp.concatenate(
            [jnp.concatenate([ref[:, at] for ref in others], axis=0) for at in lanes], axis=1
        )
        term = jnp.dot(turned[...], other, preferred_element_type=F32) * rescale
        for j in range(SIDE):
            outs[i][j, :width] = term[:, j * per : (j + 1) * per].astype(BF16)
            if with_encodings:
                at = pl.ds(pl.multiple_of(places[j] * ENC_ROWS, 8), ENC_SLOT)
                outs[i][j, width : width + ENC_SLOT] = total[at, :width].astype(BF16)
                outs[i][j, width + ENC_SLOT :] = total[at, width:].astype(BF16)


ENC_ROWS = ENC_WIDTH // (SIDE * SIDE)
ENC_SLOT = 64


def weight_term(blocks, rows, others, rescale, name, encs=None, grads=None):
    count, tokens, width = rows.shape
    d = others[0].shape[1]
    per = d // (SIDE * SIDE)
    with_encodings = encs is not None
    height = width + 2 * ENC_SLOT if with_encodings else width
    whole = pl.BlockSpec(memory_space=pltpu.VMEM)
    scratch = [pltpu.VMEM((width, count * tokens), BF16)]
    operands = [rows, *others]
    flops = 2 * count * tokens * width * d
    if with_encodings:
        scratch += [pltpu.VMEM((ENC_WIDTH + 8, 2 * width), F32)]
        operands += [*encs, grads]
        flops += 2 * grads.size * ENC_WIDTH
    return pl.pallas_call(
        functools.partial(weight_kernel, rescale, with_encodings),
        in_specs=[pl.BlockSpec(memory_space=pltpu.SMEM)] + [whole] * len(operands),
        out_specs=[whole] * SIDE,
        scratch_shapes=scratch,
        out_shape=[jax.ShapeDtypeStruct((SIDE, height, per), BF16)] * SIDE,
        compiler_params=pltpu.CompilerParams(vmem_limit_bytes=(20 if with_encodings else 10) * MB),
        cost_estimate=pl.CostEstimate(
            flops=flops, bytes_accessed=2 * d * (count * tokens + width), transcendentals=0
        ),
        name=name,
    )(blocks, *operands)


def request_tables(nbr_shard, nbr_row):
    mine = jnp.stack([nbr_shard.reshape(-1), nbr_row.reshape(-1)]).astype(jnp.int32)
    line = jnp.stack([mine] + [along_x(mine, SIDE - i) for i in range(1, SIDE)])
    return jnp.stack([line] + [along_y(line, SIDE - j) for j in range(1, SIDE)], axis=1)


def take_rows(array, index):
    return array.at[index].get(mode="promise_in_bounds")


def fetch_encodings(tables, database, nbr_shard, x, y):
    requests = nbr_shard.shape[0] * NEIGHBOURS
    slice_len = database.shape[1]
    shard_flat = nbr_shard.reshape(requests)
    me = x * SIDE + y
    wanted = tables[:, :, 0] == me
    order = jnp.arange(requests, dtype=jnp.int32)
    before = (order[None, :] < order[:, None]).astype(F32)
    slot = jnp.einsum("ijs,rs->ijr", wanted.astype(F32), before)
    slots = jnp.arange(CAPACITY, dtype=jnp.int32)
    chosen = wanted[:, :, None, :] & (
        slot[:, :, None, :].astype(jnp.int32) == slots[None, None, :, None]
    )
    rows = jnp.sum(jnp.where(chosen, tables[:, :, 1][:, :, None, :], 0), axis=3)
    rows = jnp.roll(rows, (x, y), axis=(0, 1))
    served = take_rows(database, rows.reshape(-1))
    came = lax.all_to_all(served, "db", split_axis=0, concat_axis=0, tiled=True)
    same = (shard_flat[:, None] == shard_flat[None, :]) & (order[None, :] < order[:, None])
    slot_index = jnp.sum(same.astype(jnp.int32), axis=1)
    picked = take_rows(came, shard_flat * CAPACITY + slot_index)
    return picked.reshape(requests * slice_len, ENC_WIDTH)


def per_device(hidden, grad_out, w_query, w_key, w_value, w_out, database, nbr_shard, nbr_row):
    db = lax.axis_index("db")
    seq = lax.axis_index("seq")
    x, y = db // SIDE, db % SIDE
    z, core = seq // CORES, seq % CORES
    spans = nbr_shard.shape[0]
    width = w_query.shape[1]
    token_rows = hidden.shape[0]
    total_tokens = token_rows * lax.axis_size("db") * lax.axis_size("seq")
    rescale = float(total_tokens) ** (-0.5)
    block = jnp.arange(CHIPS * CORES, dtype=jnp.int32)
    places = jnp.argmax(piece_blocks(z, core)[None, :] == block[:, None], axis=1).astype(jnp.int32)
    i, j = jnp.arange(SIDE)[:, None], jnp.arange(SIDE)[None, :]
    blocks = jnp.where(
        core == 0,
        ((x + i) % SIDE) * SIDE + (y + j) % SIDE,
        ((x + j) % SIDE) * SIDE + (y + i) % SIDE,
    )
    blocks = blocks.reshape(-1).astype(jnp.int32)

    tables = request_tables(nbr_shard, nbr_row)
    hidden_low = along_z(hidden)
    hidden_high = along_z(hidden, -1)
    grad_rows = after(grad_out, tables)
    grad_low = along_z(grad_rows)
    grad_high = along_z(grad_rows, -1)
    hidden_far = along_z(hidden_low)
    encoded = fetch_encodings(tables, database, nbr_shard, x, y)
    grad_far = along_z(grad_low)
    enc_rows = after(encoded, hidden_high, grad_high)
    enc_low = along_z(enc_rows)
    enc_high = along_z(enc_rows, -1)
    hidden_far = after(hidden_far, encoded)
    hidden_own = jnp.concatenate([hidden, hidden_far, hidden_high, hidden_low], axis=0)
    hidden_all = [hidden_own, other_core(hidden_own)]
    grad_own = jnp.concatenate([grad_out, grad_far, grad_high, grad_low], axis=0)
    grad_all = [grad_own, other_core(grad_own)]
    w_both = jnp.concatenate([w_query, other_core(after(w_query, hidden_far))], axis=1)

    pieces = 2 * CHIPS
    w_late, grad_late = after((w_query, w_out), enc_low)
    query = jnp.concatenate(
        [jnp.dot(rows, w_late, preferred_element_type=F32).astype(BF16) for rows in hidden_all]
    ).reshape(pieces, token_rows, width)
    gctx = jnp.concatenate([nt(rows, grad_late).astype(BF16) for rows in grad_all])
    gctx = gctx.reshape(pieces, token_rows, width)
    enc_far = along_z(enc_low)
    enc_all = [encoded, enc_far, enc_high, enc_low]
    enc_all += [other_core(piece) for piece in enc_all]
    w_kv = jnp.concatenate([w_key, w_value], axis=1)
    kv = [
        jnp.dot(piece, w_kv, preferred_element_type=F32).astype(BF16).reshape(spans, -1, 2 * width)
        for piece in enc_all
    ]
    context, grad_query, grad_kv = attention(places, query, gctx, kv)

    joined = jnp.concatenate([grad_query[:4], other_core(grad_query[4:])], axis=2)
    out_term = weight_term(
        blocks,
        context,
        grad_all,
        rescale,
        "out_term",
        enc_all,
        grad_kv.reshape(8, -1, 2 * width),
    )
    joined = after(joined, out_term[0])
    far = nt(joined[1], w_both).astype(BF16)
    from_far = along_z(far)
    back = nt(joined[3], w_both).astype(BF16)
    from_back = along_z(after(back, from_far), -1)
    query_term = weight_term(
        blocks, after(grad_query, far, back), hidden_all, rescale, "query_term"
    )
    near = (nt(joined[2], w_both) + from_far.astype(F32)).astype(BF16)
    from_near = along_z(near)
    query_term = list(after(tuple(query_term), near))
    own = after(nt(joined[0], w_both) + from_back.astype(F32), near)
    grad_hidden = (own + from_near.astype(F32)).astype(BF16)

    totals = [reduce_lines(query_term, 0).astype(BF16), reduce_lines(out_term, 0).astype(BF16)]
    terms = jnp.concatenate(totals, axis=1)
    arrived = [terms[0]] + [spread(terms[i], i, 1) for i in range(1, SIDE)]
    rest = sum(a.astype(F32) for a in after(arrived, grad_hidden))
    grad_w_query, grad_w_out, rest = rest[:width].T, rest[width : 2 * width], rest[2 * width :]
    grad_w_key, grad_w_value = rest[:ENC_ROWS], rest[ENC_SLOT : ENC_SLOT + ENC_ROWS]
    return grad_hidden, grad_w_query, grad_w_key, grad_w_value, grad_w_out


def solution(mesh):
    return jax.shard_map(
        per_device,
        mesh=mesh,
        in_specs=(
            P(("db", "seq"), None),
            P(("db", "seq"), None),
            P(None, "seq"),
            P(None, "seq"),
            P(None, "seq"),
            P("seq", None),
            P("db", "seq", None),
            P("db", None),
            P("db", None),
        ),
        out_specs=(
            P(("db", "seq"), None),
            P("db", "seq"),
            P("db", "seq"),
            P("db", "seq"),
            P("seq", "db"),
        ),
        check_vma=False,
    )
```
